32 devices in a mesh: row: 8 (over y, x, core), col: 4 (over z).
Axes of the slice: x: 2, y: 2, z: 4, core: 2. Of those that a mesh axis runs over, the one named last changes fastest.
Arguments:
- tokens: bfloat16 [4096, 6144], P('row', 'col'), may hold values from -6 to 6
- gate_weight: bfloat16 [6144, 12288], P('row', 'col'), may hold values from -0.078125 to 0.078125
- up_weight: bfloat16 [6144, 12288], P('row', 'col'), may hold values from -0.078125 to 0.078125
Outputs:
- hidden: float32 [4096, 12288], P('row', 'col')
The draws below stay inside these ranges and needn't reach their ends.
All inputs are finite; a program needn't handle non-finite values.
Results may differ from the reference program's by a relative error of at most 0.0003.
Values may be sent and summed in bfloat16 or wider, within the bound.
A program may use at most 192 MiB of HBM per device.

```python
import jax
import jax.numpy as jnp

D = 6144
FFW = 12288
TOKENS = 4096


def block_scale(rng, dims, shards, low, largest):
    gain = 1.0
    for axis_at, shards_of in shards:
        steps = jax.random.uniform(jax.random.fold_in(jax.random.fold_in(rng, 6), axis_at), (shards_of,), jnp.float32, low / len(shards), largest / len(shards))
        gain = gain * jnp.repeat(jnp.exp(steps), dims[axis_at] // shards_of).reshape((-1,) + (1,) * (len(dims) - 1 - axis_at))
    return gain


def normal_values(rng, shape, width, limit, pieces=(), held_as=jnp.bfloat16):
    factor_of = block_scale(rng, shape, pieces, -0.22, 0.18) if pieces else 1.0
    drawn = jax.random.normal(rng, shape, jnp.float32) * width * factor_of
    return jnp.minimum(jnp.maximum(drawn, -limit), limit).astype(held_as)


def setup_inputs(seed: int = 0) -> dict:
    streams_of = jax.random.split(jax.random.key(seed), 4)
    tokens = normal_values(streams_of[0], (TOKENS, D), 1.0, 6.0, ((0, 8), (1, 4)))
    gate_weight = normal_values(streams_of[1], (D, FFW), D ** -0.5, 0.078125, ((0, 8), (1, 4)))
    up_weight = normal_values(streams_of[2], (D, FFW), D ** -0.5, 0.078125, ((0, 8), (1, 4)))
    return dict(tokens=tokens, gate_weight=gate_weight, up_weight=up_weight)


def reference(tokens, gate_weight, up_weight):
    gate_sum = jnp.dot(tokens, gate_weight, preferred_element_type=jnp.float32)
    up_sum = jnp.dot(tokens, up_weight, preferred_element_type=jnp.float32)
    return jax.nn.silu(gate_sum) * up_sum
```

```python
import functools

import jax
import jax.numpy as jnp
from jax import lax
from jax.experimental import pallas as pl
from jax.experimental.pallas import tpu as pltpu
from jax.sharding import PartitionSpec as P

MESH = pl.DeviceIdType.MESH


def kernel(Y, X, Z, n, tok, gate, up, out, T, W, O, loc, sibs, sibr, tls, tlr, ts, tr, tfs, tfr,
           xs, xr, ys, yr, fas, far, fbs, fbr, ol, osd, orv, tl):
    rows, kz = tok.shape
    kr = gate.shape[0]
    half = gate.shape[1] // 2
    J = half // n
    row, z = lax.axis_index("row"), lax.axis_index("col")
    c, p = lax.rem(row, 2), row // 2
    x, y = lax.rem(p, X), p // X
    sib = row + 1 - 2 * c
    kc = 2 * kr

    def chip(yy, xx):
        return yy * X + xx

    def al(v, k):
        return pl.multiple_of(v, k)

    def remote(src, dst, s, r, drow, dcol):
        return pltpu.make_async_remote_copy(
            src_ref=src, dst_ref=dst, send_sem=s, recv_sem=r,
            device_id=(drow, dcol), device_id_type=MESH)

    def block(j, q):
        return W.at[j, pl.ds(al(q * kc, kc), kc), :]

    def part(j, q, h):
        return W.at[j, pl.ds(al(q * kc + h * kr, kr), kr), :]

    xpeers = [lax.rem(x + d, X) for d in range(1, X)]
    xfrom = [lax.rem(x + X - d, X) for d in range(1, X)]
    ypeers = [lax.rem(y + d, Y) for d in range(1, Y)]
    yfrom = [lax.rem(y + Y - d, Y) for d in range(1, Y)]
    zpeers = [lax.rem(z + d, Z) for d in range(1, Z)]
    zfrom = [lax.rem(z + Z - d, Z) for d in range(1, Z)]

    barrier = pltpu.get_barrier_semaphore()
    peers = [(sib, z)] + [(row, q) for q in zpeers]
    peers += [(chip(y, q) * 2 + c, z) for q in xpeers]
    peers += [(chip(q, x) * 2 + c, z) for q in ypeers]
    for q in peers:
        pl.semaphore_signal(barrier, inc=1, device_id=q, device_id_type=MESH)
    pl.semaphore_wait(barrier, len(peers))

    def local_copies(j):
        return [
            pltpu.make_async_copy(
                ref.at[:, pl.ds(al(c * half + j * n, n), n)],
                W.at[j, pl.ds(al(row * kr, kr), kr), pl.ds(i * n, n)],
                loc.at[j, i])
            for i, ref in enumerate((gate, up))]

    def sib_copies(j, owner, other):
        return [
            remote(
                ref.at[:, pl.ds(al(other * half + j * n, n), n)],
                W.at[j, pl.ds(al(owner * kr, kr), kr), pl.ds(i * n, n)],
                sibs.at[j, i], sibr.at[j, i], sib, z)
            for i, ref in enumerate((gate, up))]

    def fetch(j):
        for k in local_copies(j) + sib_copies(j, row, 1 - c):
            k.start()

    def xdirect(j, d, q):
        return remote(block(j, q), block(j, q), xs.at[j, d], xr.at[j, d],
                      chip(y, xpeers[d]) * 2 + c, z)

    def ydirect(j, d, q):
        return remote(block(j, q), block(j, q), ys.at[j, d], yr.at[j, d],
                      chip(ypeers[d], x) * 2 + c, z)

    def fwda(j, dx, dy, q):
        return remote(part(j, q, 0), part(j, q, 0), fas.at[j, dx, dy], far.at[j, dx, dy],
                      chip(ypeers[dy], x) * 2 + c, z)

    def fwdb(j, dx, dy, q):
        return remote(part(j, q, 1), part(j, q, 1), fbs.at[j, dx, dy], fbr.at[j, dx, dy],
                      chip(y, xpeers[dx]) * 2 + c, z)

    def trows(q, core):
        return T.at[q, pl.ds(al(core * rows, rows), rows), :]

    tok_local = pltpu.make_async_copy(tok, trows(z, c), tl.at[0])
    tok_sib = remote(tok, trows(z, c), tls.at[0], tlr.at[0], sib, z)
    tok_send = [remote(tok, trows(z, c), ts.at[d], tr.at[d], row, zpeers[d]) for d in range(Z - 1)]

    def tok_fwd(d, core):
        return remote(trows(zfrom[d], core), trows(zfrom[d], core), tfs.at[d], tfr.at[d], sib, z)

    def out_local(j):
        return pltpu.make_async_copy(
            O.at[j, pl.ds(al(c * rows, rows), rows), :],
            out.at[:, pl.ds(al(c * half + j * n, n), n)], ol.at[j])

    def out_sib(j, core):
        return remote(
            O.at[j, pl.ds(al((1 - c) * rows, rows), rows), :],
            out.at[:, pl.ds(al(core * half + j * n, n), n)], osd.at[j], orv.at[j], sib, z)

    fetch(0)
    for k in tok_send:
        k.start()
    if J > 1:
        fetch(1)
    tok_local.start()
    tok_sib.start()

    late = (J + 1) // 2

    def done(s):
        return jnp.maximum(jnp.minimum(s - 1, 2 * (s - late + 1)), 0)

    def compute(j, carry):
        for d in range(X - 1):
            for e in range(Y - 1):
                q = chip(yfrom[e], xfrom[d])
                fwda(j, d, e, q).wait_recv()
                fwdb(j, d, e, q).wait_recv()

        def tile(m, carry):
            r = pl.ds(al(m * rows, rows), rows)
            total = jnp.zeros((rows, 2 * n), jnp.float32)
            for q in range(Z):
                total += jnp.dot(T[q, r, :], W[j, q * kz:(q + 1) * kz, :],
                                 preferred_element_type=jnp.float32)
            g, u = total[:, :n], total[:, n:]
            O[j, r, :] = g / (1.0 + jnp.exp(-g)) * u
            return carry

        lax.fori_loop(0, 2, tile, 0)
        out_local(j).start()
        out_sib(j, c).start()
        return carry

    def step(s, carry):
        @pl.when(s < J)
        def _():
            for k in local_copies(s):
                k.wait()
            for k in sib_copies(s, sib, 1 - c):
                k.wait_recv()
            for d in range(X - 1):
                xdirect(s, d, p).start()
            for d in range(Y - 1):
                ydirect(s, d, p).start()

        @pl.when(s + 2 < J)
        def _():
            fetch(s + 2)

        @pl.when(jnp.logical_and(s >= 1, s <= J))
        def _():
            j = s - 1
            for d in range(X - 1):
                q = chip(y, xfrom[d])
                xdirect(j, d, q).wait_recv()
                for e in range(Y - 1):
                    fwda(j, d, e, q).start()
            for e in range(Y - 1):
                q = chip(yfrom[e], x)
                ydirect(j, e, q).wait_recv()
                for d in range(X - 1):
                    fwdb(j, d, e, q).start()

        @pl.when(s == late - 1)
        def _():
            for d in range(Z - 1):
                tok_send[d].wait_recv()
                tok_fwd(d, c).start()

        @pl.when(s == late)
        def _():
            tok_local.wait()
            remote(tok, trows(z, 1 - c), tls.at[0], tlr.at[0], sib, z).wait_recv()
            for d in range(Z - 1):
                tok_fwd(d, 1 - c).wait_recv()

        lax.fori_loop(done(s - 1), done(s), compute, 0)
        return carry

    lax.fori_loop(0, J + 2, step, 0)

    tok_sib.wait_send()
    for d in range(Z - 1):
        tok_send[d].wait_send()
        tok_fwd(d, c).wait_send()

    def finish(j, carry):
        for k in sib_copies(j, row, 1 - c):
            k.wait_send()
        for d in range(X - 1):
            xdirect(j, d, p).wait_send()
            for e in range(Y - 1):
                fwda(j, d, e, chip(y, xfrom[d])).wait_send()
        for e in range(Y - 1):
            ydirect(j, e, p).wait_send()
            for d in range(X - 1):
                fwdb(j, d, e, chip(yfrom[e], x)).wait_send()
        out_local(j).wait()
        out_sib(j, c).wait_send()
        out_sib(j, 1 - c).wait_recv()
        return carry

    lax.fori_loop(0, J, finish, 0)


def solution(mesh):
    R, Z = mesh.shape["row"], mesh.shape["col"]
    chips = R // 2
    Y = 2 if chips % 2 == 0 else 1
    X = chips // Y

    def per_device(tokens, gate_weight, up_weight):
        rows, kz = tokens.shape
        kr, cols = gate_weight.shape
        n = 128
        half = cols // 2
        J = half // n
        dma = pltpu.SemaphoreType.DMA
        ux, uy, uz = max(X - 1, 1), max(Y - 1, 1), max(Z - 1, 1)
        scratch = [
            pltpu.VMEM((Z, 2 * rows, kz), jnp.bfloat16),
            pltpu.VMEM((J, R * kr, 2 * n), jnp.bfloat16),
            pltpu.VMEM((J, 2 * rows, n), jnp.float32),
            dma((J, 2)), dma((J, 2)), dma((J, 2)),
            dma((1,)), dma((1,)), dma((uz,)), dma((uz,)), dma((uz,)), dma((uz,)),
            dma((J, ux)), dma((J, ux)), dma((J, uy)), dma((J, uy)),
            dma((J, ux, uy)), dma((J, ux, uy)), dma((J, ux, uy)), dma((J, ux, uy)),
            dma((J,)), dma((J,)), dma((J,)), dma((1,)),
        ]
        return pl.pallas_call(
            functools.partial(kernel, Y, X, Z, n),
            out_shape=jax.ShapeDtypeStruct((rows, cols), jnp.float32),
            in_specs=[pl.BlockSpec(memory_space=pl.ANY)] * 3,
            out_specs=pl.BlockSpec(memory_space=pl.ANY),
            scratch_shapes=scratch,
            compiler_params=pltpu.CompilerParams(
                collective_id=0, has_side_effects=True, vmem_limit_bytes=62 * 2**20),
            cost_estimate=pl.CostEstimate(
                flops=4 * rows * R * kr * cols, bytes_accessed=4 * rows * cols,
                transcendentals=rows * cols),
        )(tokens, gate_weight, up_weight)

    return jax.shard_map(
        per_device, mesh=mesh, in_specs=(P("row", "col"),) * 3,
        out_specs=P("row", "col"), check_vma=False)
```

```python
import functools

import jax
import jax.numpy as jnp
from jax import lax
from jax.experimental import pallas as pl
from jax.experimental.pallas import tpu as pltpu
from jax.sharding import PartitionSpec as P

MESH = pl.DeviceIdType.MESH


def kernel(Y, X, Z, n, tok, gate, up, out, T, W, O, loc, sibs, sibr, tls, tlr, ts, tr, tfs, tfr,
           xs, xr, ys, yr, fas, far, fbs, fbr, ol, osd, orv, tl):
    rows, kz = tok.shape
    kr = gate.shape[0]
    half = gate.shape[1] // 2
    J = half // n
    row, z = lax.axis_index("row"), lax.axis_index("col")
    c, p = lax.rem(row, 2), row // 2
    x, y = lax.rem(p, X), p // X
    sib = row + 1 - 2 * c
    kc = 2 * kr

    def chip(yy, xx):
        return yy * X + xx

    def al(v, k):
        return pl.multiple_of(v, k)

    def remote(src, dst, s, r, drow, dcol):
        return pltpu.make_async_remote_copy(
            src_ref=src, dst_ref=dst, send_sem=s, recv_sem=r,
            device_id=(drow, dcol), device_id_type=MESH)

    def block(j, q):
        return W.at[j, pl.ds(al(q * kc, kc), kc), :]

    def part(j, q, h):
        return W.at[j, pl.ds(al(q * kc + h * kr, kr), kr), :]

    xpeers = [lax.rem(x + d, X) for d in range(1, X)]
    xfrom = [lax.rem(x + X - d, X) for d in range(1, X)]
    ypeers = [lax.rem(y + d, Y) for d in range(1, Y)]
    yfrom = [lax.rem(y + Y - d, Y) for d in range(1, Y)]
    zpeers = [lax.rem(z + d, Z) for d in range(1, Z)]
    zfrom = [lax.rem(z + Z - d, Z) for d in range(1, Z)]

    barrier = pltpu.get_barrier_semaphore()
    peers = [(sib, z)] + [(row, q) for q in zpeers]
    peers += [(chip(y, q) * 2 + c, z) for q in xpeers]
    peers += [(chip(q, x) * 2 + c, z) for q in ypeers]
    for q in peers:
        pl.semaphore_signal(barrier, inc=1, device_id=q, device_id_type=MESH)
    pl.semaphore_wait(barrier, len(peers))

    def local_copies(j):
        return [
            pltpu.make_async_copy(
                ref.at[:, pl.ds(al(c * half + j * n, n), n)],
                W.at[j, pl.ds(al(row * kr, kr), kr), pl.ds(i * n, n)],
                loc.at[j, i])
            for i, ref in enumerate((gate, up))]

    def sib_copies(j, owner, other):
        return [
            remote(
                ref.at[:, pl.ds(al(other * half + j * n, n), n)],
                W.at[j, pl.ds(al(owner * kr, kr), kr), pl.ds(i * n, n)],
                sibs.at[j, i], sibr.at[j, i], sib, z)
            for i, ref in enumerate((gate, up))]

    def fetch(j):
        for k in local_copies(j) + sib_copies(j, row, 1 - c):
            k.start()

    def xdirect(j, d, q):
        return remote(block(j, q), block(j, q), xs.at[j, d], xr.at[j, d],
                      chip(y, xpeers[d]) * 2 + c, z)

    def ydirect(j, d, q):
        return remote(block(j, q), block(j, q), ys.at[j, d], yr.at[j, d],
                      chip(ypeers[d], x) * 2 + c, z)

    def fwda(j, dx, dy, q):
        return remote(part(j, q, 0), part(j, q, 0), fas.at[j, dx, dy], far.at[j, dx, dy],
                      chip(ypeers[dy], x) * 2 + c, z)

    def fwdb(j, dx, dy, q):
        return remote(part(j, q, 1), part(j, q, 1), fbs.at[j, dx, dy], fbr.at[j, dx, dy],
                      chip(y, xpeers[dx]) * 2 + c, z)

    def trows(q, core):
        return T.at[q, pl.ds(al(core * rows, rows), rows), :]

    tok_local = pltpu.make_async_copy(tok, trows(z, c), tl.at[0])
    tok_sib = remote(tok, trows(z, c), tls.at[0], tlr.at[0], sib, z)
    tok_send = [remote(tok, trows(z, c), ts.at[d], tr.at[d], row, zpeers[d]) for d in range(Z - 1)]

    def tok_fwd(d, core):
        return remote(trows(zfrom[d], core), trows(zfrom[d], core), tfs.at[d], tfr.at[d], sib, z)

    def out_local(j):
        return pltpu.make_async_copy(
            O.at[j, pl.ds(al(c * rows, rows), rows), :],
            out.at[:, pl.ds(al(c * half + j * n, n), n)], ol.at[j])

    def out_sib(j, core):
        return remote(
            O.at[j, pl.ds(al((1 - c) * rows, rows), rows), :],
            out.at[:, pl.ds(al(core * half + j * n, n), n)], osd.at[j], orv.at[j], sib, z)

    fetch(0)
    for k in tok_send:
        k.start()
    if J > 1:
        fetch(1)
    tok_local.start()
    tok_sib.start()

    late = (J + 1) // 2

    def done(s):
        return jnp.maximum(jnp.minimum(s - 1, 2 * (s - late + 1)), 0)

    def compute(j, carry):
        for d in range(X - 1):
            for e in range(Y - 1):
                q = chip(yfrom[e], xfrom[d])
                fwda(j, d, e, q).wait_recv()
                fwdb(j, d, e, q).wait_recv()

        def tile(m, carry):
            r = pl.ds(al(m * rows, rows), rows)
            total = jnp.zeros((rows, 2 * n), jnp.float32)
            for q in range(Z):
                total += jnp.dot(T[q, r, :], W[j, q * kz:(q + 1) * kz, :],
                                 preferred_element_type=jnp.float32)
            g, u = total[:, :n], total[:, n:]
            O[j, r, :] = g / (1.0 + jnp.exp(-g)) * u
            return carry

        lax.fori_loop(0, 2, tile, 0)
        out_local(j).start()
        out_sib(j, c).start()
        return carry

    def step(s, carry):
        @pl.when(s < J)
        def _():
            for k in local_copies(s):
                k.wait()
            for k in sib_copies(s, sib, 1 - c):
                k.wait_recv()
            for d in range(X - 1):
                xdirect(s, d, p).start()
            for d in range(Y - 1):
                ydirect(s, d, p).start()

        @pl.when(s + 2 < J)
        def _():
            fetch(s + 2)

        @pl.when(jnp.logical_and(s >= 1, s <= J))
        def _():
            j = s - 1
            for d in range(X - 1):
                q = chip(y, xfrom[d])
                xdirect(j, d, q).wait_recv()
                for e in range(Y - 1):
                    fwda(j, d, e, q).start()
            for e in range(Y - 1):
                q = chip(yfrom[e], x)
                ydirect(j, e, q).wait_recv()
                for d in range(X - 1):
                    fwdb(j, d, e, q).start()

        @pl.when(s == late - 1)
        def _():
            for d in range(Z - 1):
                tok_send[d].wait_recv()
                tok_fwd(d, c).start()

        @pl.when(s == late)
        def _():
            tok_local.wait()
            remote(tok, trows(z, 1 - c), tls.at[0], tlr.at[0], sib, z).wait_recv()
            for d in range(Z - 1):
                tok_fwd(d, 1 - c).wait_recv()

        lax.fori_loop(done(s - 1), done(s), compute, 0)
        return carry

    lax.fori_loop(0, J + 2, step, 0)

    tok_sib.wait_send()
    for d in range(Z - 1):
        tok_send[d].wait_send()
        tok_fwd(d, c).wait_send()

    def finish(j, carry):
        for k in sib_copies(j, row, 1 - c):
            k.wait_send()
        for d in range(X - 1):
            xdirect(j, d, p).wait_send()
            for e in range(Y - 1):
                fwda(j, d, e, chip(y, xfrom[d])).wait_send()
        for e in range(Y - 1):
            ydirect(j, e, p).wait_send()
            for d in range(X - 1):
                fwdb(j, d, e, chip(yfrom[e], x)).wait_send()
        out_local(j).wait()
        out_sib(j, c).wait_send()
        out_sib(j, 1 - c).wait_recv()
        return carry

    lax.fori_loop(0, J, finish, 0)


def grid_kernel(Y, X, Z, n, tok, gate, up, out, T, W, O, loc, sibs, sibr, ys, yr, xs, xr,
                tl, hs, hr, zs, zr, fs, fr, ol, osd, orv):
    rows, kz = tok.shape
    kr = gate.shape[0]
    quarter = gate.shape[1] // 4
    J = quarter // n
    kc = 2 * kr
    row, z = lax.axis_index("row"), lax.axis_index("col")
    c, p = lax.rem(row, 2), row // 2
    x, y = lax.rem(p, X), p // X
    c2, y2 = 1 - c, 1 - y

    def dev(yy, xx, cc):
        return (yy * X + xx) * 2 + cc

    def al(v, k):
        return pl.multiple_of(v, k)

    def remote(src, dst, s, r, drow, dcol):
        return pltpu.make_async_remote_copy(
            src_ref=src, dst_ref=dst, send_sem=s, recv_sem=r,
            device_id=(drow, dcol), device_id_type=MESH)

    sib, across, cross = dev(y, x, c2), dev(y2, x, c), dev(y2, x, c2)
    xpeers = [lax.rem(x + d, X) for d in range(1, X)]
    xfrom = [lax.rem(x + X - d, X) for d in range(1, X)]

    barrier = pltpu.get_barrier_semaphore()

    def greet(drow, dcol):
        pl.semaphore_signal(barrier, inc=1, device_id=(drow, dcol), device_id_type=MESH)

    for q in [sib, across, cross] + [dev(y, q, c) for q in xpeers]:
        greet(q, z)

    @pl.when(z > 0)
    def _():
        greet(row, z - 1)

    @pl.when(z < Z - 1)
    def _():
        greet(row, z + 1)

    pl.semaphore_wait(barrier, 2 + X + jnp.minimum(z, 1) + jnp.minimum(Z - 1 - z, 1))

    def cols(ref, yy, cc, j):
        return ref.at[:, pl.ds(al((yy * 2 + cc) * quarter + j * n, n), n)]

    def place(j, owner, i):
        return W.at[j, pl.ds(al(owner * kr, kr), kr), pl.ds(i * n, n)]

    def local_copies(j):
        return [pltpu.make_async_copy(cols(ref, y, c, j), place(j, row, i), loc.at[j, i])
                for i, ref in enumerate((gate, up))]

    def sib_copies(j, owner):
        return [remote(cols(ref, y, c2, j), place(j, owner, i), sibs.at[j, i], sibr.at[j, i], sib, z)
                for i, ref in enumerate((gate, up))]

    def y_copies(j, owners):
        return [remote(cols(ref, y2, cc, j), place(j, owners[k], i), ys.at[j, k, i], yr.at[j, k, i],
                       dest, z)
                for k, (cc, dest) in enumerate(((c, across), (c2, cross)))
                for i, ref in enumerate((gate, up))]

    def x_copy(j, d, k, q):
        yy = y2 if k else y
        b = W.at[j, pl.ds(al((yy * X + q) * kc, kc), kc), :]
        return remote(b, b, xs.at[j, d, k], xr.at[j, d, k], dev(y, xpeers[d], c), z)

    def fetch(j):
        for k in local_copies(j) + sib_copies(j, row) + y_copies(j, (row, row)):
            k.start()

    def trows(q, t, core):
        return T.at[q, pl.ds(al(((y if t else y2) * 2 + core) * rows, rows), rows), :]

    tok_local = pltpu.make_async_copy(tok, trows(z, 1, c), tl.at[0])
    tok_y = remote(tok, trows(z, 1, c), hs.at[0], hr.at[0], across, z)
    tok_y_in = remote(tok, trows(z, 0, c), hs.at[0], hr.at[0], across, z)
    tok_sib = remote(tok, trows(z, 1, c), hs.at[1], hr.at[1], sib, z)
    tok_sib_in = remote(tok, trows(z, 1, c2), hs.at[1], hr.at[1], sib, z)

    def pair_sib(core):
        return remote(trows(z, 0, core), trows(z, 0, core), hs.at[2], hr.at[2], sib, z)

    def hop(t, h, up_way, q):
        w = 0 if up_way else 1
        dst = z + 1 if up_way else z - 1
        src = tok if (t == 1 and h == 1) else trows(q, t, c)
        return remote(src, trows(q, t, c), zs.at[t, h - 1, w], zr.at[t, h - 1, w], row, dst)

    def has_send(h, up_way):
        return (jnp.logical_and(z >= h - 1, z < Z - 1) if up_way
                else jnp.logical_and(z <= Z - h, z > 0))

    def has_recv(h, up_way):
        return z >= h if up_way else z < Z - h

    def hop_send(t, h, wait=False):
        for up_way in (True, False):
            @pl.when(has_send(h, up_way))
            def _():
                q = z - (h - 1) if up_way else z + (h - 1)
                k = hop(t, h, up_way, q)
                if wait:
                    k.wait_send()
                else:
                    k.start()

    def to_sib(t, h, up_way, core):
        q = z - h if up_way else z + h
        w = 0 if up_way else 1
        return remote(trows(q, t, core), trows(q, t, core), fs.at[t, h - 1, w], fr.at[t, h - 1, w], sib, z)

    def hop_recv(t, h):
        for up_way in (True, False):
            @pl.when(has_recv(h, up_way))
            def _():
                q = z - h if up_way else z + h
                hop(t, h, up_way, q).wait_recv()
                to_sib(t, h, up_way, c).start()

            if h < Z - 1:
                @pl.when(has_send(h + 1, up_way))
                def _():
                    hop(t, h + 1, up_way, z - h if up_way else z + h).start()

    def sib_wait(t, send):
        for h in range(1, Z):
            for up_way in (True, False):
                @pl.when(has_recv(h, up_way))
                def _():
                    if send:
                        to_sib(t, h, up_way, c).wait_send()
                    else:
                        to_sib(t, h, up_way, c2).wait_recv()

    def orows(j, yy, cc):
        return O.at[j, pl.ds(al((yy * 2 + cc) * rows, rows), rows), :]

    def out_local(j):
        return pltpu.make_async_copy(orows(j, y, c), cols(out, y, c, j), ol.at[j])

    def out_copy(j, k, incoming=False):
        yy, cc, dest = ((y, c2, sib), (y2, c, across), (y2, c2, cross))[k]
        fy, fc = (yy, cc) if incoming else (y, c)
        return remote(orows(j, yy, cc), cols(out, fy, fc, j), osd.at[j, k], orv.at[j, k], dest, z)

    def tiles(j, yy):
        def tile(m, carry):
            r = pl.ds(al((yy * 2 + m) * rows, rows), rows)
            total = jnp.zeros((rows, 2 * n), jnp.float32)
            for q in range(Z):
                total += jnp.dot(T[q, r, :], W[j, q * kz:(q + 1) * kz, :],
                                 preferred_element_type=jnp.float32)
            g, u = total[:, :n], total[:, n:]
            O[j, r, :] = g / (1.0 + jnp.exp(-g)) * u
            return carry

        lax.fori_loop(0, 2, tile, 0)

    def compute_pair(j, carry):
        tiles(j, y2)
        out_copy(j, 1).start()
        out_copy(j, 2).start()
        return carry

    def compute_own(j, carry):
        tiles(j, y)
        out_local(j).start()
        out_copy(j, 0).start()
        return carry

    tok_y.start()
    fetch(0)
    tok_local.start()
    tok_sib.start()
    fetch(1)

    def done(s):
        return jnp.where(s < Z - 1, 0, s)

    def step(s, carry):
        @pl.when(s < J)
        def _():
            for k in local_copies(s):
                k.wait()
            for k in sib_copies(s, sib):
                k.wait_recv()
            for d in range(X - 1):
                x_copy(s, d, 0, x).start()

        @pl.when(s + 2 < J)
        def _():
            fetch(s + 2)

        @pl.when(s == 0)
        def _():
            tok_y_in.wait_recv()
            hop_send(0, 1)
            pair_sib(c).start()

        @pl.when(s < J)
        def _():
            for k in y_copies(s, (across, cross)):
                k.wait_recv()
            for d in range(X - 1):
                x_copy(s, d, 1, x).start()

        for h in range(1, Z):
            @pl.when(s == h)
            def _():
                hop_recv(0, h)
                if h == max(Z - 2, 1):
                    hop_send(1, 1)

        for h in range(1, Z):
            @pl.when(s == (J if h == Z - 1 else Z - 2 + h))
            def _():
                hop_recv(1, h)

        @pl.when(s == Z - 1)
        def _():
            pair_sib(c2).wait_recv()
            sib_wait(0, False)

        @pl.when(s == J)
        def _():
            tok_local.wait()
            tok_sib_in.wait_recv()
            sib_wait(1, False)

        lax.fori_loop(0, jnp.where(s == J, J - 1, 0), compute_own, 0)

        @pl.when(s >= 1)
        def _():
            for d in range(X - 1):
                for k in range(2):
                    x_copy(s - 1, d, k, xfrom[d]).wait_recv()

        lax.fori_loop(done(s - 1), done(s), compute_pair, 0)
        return carry

    lax.fori_loop(0, J + 1, step, 0)
    compute_own(J - 1, 0)

    tok_y.wait_send()
    tok_sib.wait_send()
    pair_sib(c).wait_send()
    for t in range(2):
        sib_wait(t, True)
        for h in range(1, Z):
            hop_send(t, h, wait=True)

    def finish(j, carry):
        for k in sib_copies(j, row) + y_copies(j, (row, row)):
            k.wait_send()
        for d in range(X - 1):
            for k in range(2):
                x_copy(j, d, k, x).wait_send()
        out_local(j).wait()
        for k in range(3):
            out_copy(j, k).wait_send()
            out_copy(j, k, True).wait_recv()
        return carry

    lax.fori_loop(0, J, finish, 0)


def solution(mesh):
    R, Z = mesh.shape["row"], mesh.shape["col"]
    chips = R // 2
    Y = 2 if chips % 2 == 0 else 1
    X = chips // Y

    def per_device(tokens, gate_weight, up_weight):
        rows, kz = tokens.shape
        kr, cols = gate_weight.shape
        n = 128
        half = cols // 2
        J = half // n
        dma = pltpu.SemaphoreType.DMA
        ux, uy, uz = max(X - 1, 1), max(Y - 1, 1), max(Z - 1, 1)
        quarter = cols // 4
        grid = Y == 2 and Z > 2 and quarter % n == 0 and quarter // n >= 2 * Z - 2
        scratch = [
            pltpu.VMEM((Z, 2 * rows, kz), jnp.bfloat16),
            pltpu.VMEM((J, R * kr, 2 * n), jnp.bfloat16),
            pltpu.VMEM((J, 2 * rows, n), jnp.float32),
            dma((J, 2)), dma((J, 2)), dma((J, 2)),
            dma((1,)), dma((1,)), dma((uz,)), dma((uz,)), dma((uz,)), dma((uz,)),
            dma((J, ux)), dma((J, ux)), dma((J, uy)), dma((J, uy)),
            dma((J, ux, uy)), dma((J, ux, uy)), dma((J, ux, uy)), dma((J, ux, uy)),
            dma((J,)), dma((J,)), dma((J,)), dma((1,)),
        ]
        if grid:
            J = quarter // n
            scratch = [
                pltpu.VMEM((Z, 4 * rows, kz), jnp.bfloat16),
                pltpu.VMEM((J, R * kr, 2 * n), jnp.bfloat16),
                pltpu.VMEM((J, 4 * rows, n), jnp.float32),
                dma((J, 2)), dma((J, 2)), dma((J, 2)), dma((J, 2, 2)), dma((J, 2, 2)),
                dma((J, ux, 2)), dma((J, ux, 2)), dma((1,)), dma((3,)), dma((3,)),
                dma((2, uz, 2)), dma((2, uz, 2)), dma((2, uz, 2)), dma((2, uz, 2)),
                dma((J,)), dma((J, 3)), dma((J, 3)),
            ]
        return pl.pallas_call(
            functools.partial(grid_kernel if grid else kernel, Y, X, Z, n),
            out_shape=jax.ShapeDtypeStruct((rows, cols), jnp.float32),
            in_specs=[pl.BlockSpec(memory_space=pl.ANY)] * 3,
            out_specs=pl.BlockSpec(memory_space=pl.ANY),
            scratch_shapes=scratch,
            compiler_params=pltpu.CompilerParams(
                collective_id=0, has_side_effects=True, vmem_limit_bytes=62 * 2**20),
            cost_estimate=pl.CostEstimate(
                flops=4 * rows * R * kr * cols, bytes_accessed=4 * rows * cols,
                transcendentals=rows * cols),
        )(tokens, gate_weight, up_weight)

    return jax.shard_map(
        per_device, mesh=mesh, in_specs=(P("row", "col"),) * 3,
        out_specs=P("row", "col"), check_vma=False)
```

```python
import functools

import jax
import jax.numpy as jnp
from jax import lax
from jax.experimental import pallas as pl
from jax.experimental.pallas import tpu as pltpu
from jax.sharding import PartitionSpec as P

MESH = pl.DeviceIdType.MESH


def kernel(Y, X, Z, n, tok, gate, up, out, T, W, O, loc, sibs, sibr, tls, tlr, ts, tr, tfs, tfr,
           xs, xr, ys, yr, fas, far, fbs, fbr, ol, osd, orv, tl):
    rows, kz = tok.shape
    kr = gate.shape[0]
    half = gate.shape[1] // 2
    J = half // n
    row, z = lax.axis_index("row"), lax.axis_index("col")
    c, p = lax.rem(row, 2), row // 2
    x, y = lax.rem(p, X), p // X
    sib = row + 1 - 2 * c
    kc = 2 * kr

    def chip(yy, xx):
        return yy * X + xx

    def al(v, k):
        return pl.multiple_of(v, k)

    def remote(src, dst, s, r, drow, dcol):
        return pltpu.make_async_remote_copy(
            src_ref=src, dst_ref=dst, send_sem=s, recv_sem=r,
            device_id=(drow, dcol), device_id_type=MESH)

    def block(j, q):
        return W.at[j, pl.ds(al(q * kc, kc), kc), :]

    def part(j, q, h):
        return W.at[j, pl.ds(al(q * kc + h * kr, kr), kr), :]

    xpeers = [lax.rem(x + d, X) for d in range(1, X)]
    xfrom = [lax.rem(x + X - d, X) for d in range(1, X)]
    ypeers = [lax.rem(y + d, Y) for d in range(1, Y)]
    yfrom = [lax.rem(y + Y - d, Y) for d in range(1, Y)]
    zpeers = [lax.rem(z + d, Z) for d in range(1, Z)]
    zfrom = [lax.rem(z + Z - d, Z) for d in range(1, Z)]

    barrier = pltpu.get_barrier_semaphore()
    peers = [(sib, z)] + [(row, q) for q in zpeers]
    peers += [(chip(y, q) * 2 + c, z) for q in xpeers]
    peers += [(chip(q, x) * 2 + c, z) for q in ypeers]
    for q in peers:
        pl.semaphore_signal(barrier, inc=1, device_id=q, device_id_type=MESH)
    pl.semaphore_wait(barrier, len(peers))

    def local_copies(j):
        return [
            pltpu.make_async_copy(
                ref.at[:, pl.ds(al(c * half + j * n, n), n)],
                W.at[j, pl.ds(al(row * kr, kr), kr), pl.ds(i * n, n)],
                loc.at[j, i])
            for i, ref in enumerate((gate, up))]

    def sib_copies(j, owner, other):
        return [
            remote(
                ref.at[:, pl.ds(al(other * half + j * n, n), n)],
                W.at[j, pl.ds(al(owner * kr, kr), kr), pl.ds(i * n, n)],
                sibs.at[j, i], sibr.at[j, i], sib, z)
            for i, ref in enumerate((gate, up))]

    def fetch(j):
        for k in local_copies(j) + sib_copies(j, row, 1 - c):
            k.start()

    def xdirect(j, d, q):
        return remote(block(j, q), block(j, q), xs.at[j, d], xr.at[j, d],
                      chip(y, xpeers[d]) * 2 + c, z)

    def ydirect(j, d, q):
        return remote(block(j, q), block(j, q), ys.at[j, d], yr.at[j, d],
                      chip(ypeers[d], x) * 2 + c, z)

    def fwda(j, dx, dy, q):
        return remote(part(j, q, 0), part(j, q, 0), fas.at[j, dx, dy], far.at[j, dx, dy],
                      chip(ypeers[dy], x) * 2 + c, z)

    def fwdb(j, dx, dy, q):
        return remote(part(j, q, 1), part(j, q, 1), fbs.at[j, dx, dy], fbr.at[j, dx, dy],
                      chip(y, xpeers[dx]) * 2 + c, z)

    def trows(q, core):
        return T.at[q, pl.ds(al(core * rows, rows), rows), :]

    tok_local = pltpu.make_async_copy(tok, trows(z, c), tl.at[0])
    tok_sib = remote(tok, trows(z, c), tls.at[0], tlr.at[0], sib, z)
    tok_send = [remote(tok, trows(z, c), ts.at[d], tr.at[d], row, zpeers[d]) for d in range(Z - 1)]

    def tok_fwd(d, core):
        return remote(trows(zfrom[d], core), trows(zfrom[d], core), tfs.at[d], tfr.at[d], sib, z)

    def out_local(j):
        return pltpu.make_async_copy(
            O.at[j, pl.ds(al(c * rows, rows), rows), :],
            out.at[:, pl.ds(al(c * half + j * n, n), n)], ol.at[j])

    def out_sib(j, core):
        return remote(
            O.at[j, pl.ds(al((1 - c) * rows, rows), rows), :],
            out.at[:, pl.ds(al(core * half + j * n, n), n)], osd.at[j], orv.at[j], sib, z)

    fetch(0)
    for k in tok_send:
        k.start()
    if J > 1:
        fetch(1)
    tok_local.start()
    tok_sib.start()

    late = (J + 1) // 2

    def done(s):
        return jnp.maximum(jnp.minimum(s - 1, 2 * (s - late + 1)), 0)

    def compute(j, carry):
        for d in range(X - 1):
            for e in range(Y - 1):
                q = chip(yfrom[e], xfrom[d])
                fwda(j, d, e, q).wait_recv()
                fwdb(j, d, e, q).wait_recv()

        def tile(m, carry):
            r = pl.ds(al(m * rows, rows), rows)
            total = jnp.zeros((rows, 2 * n), jnp.float32)
            for q in range(Z):
                total += jnp.dot(T[q, r, :], W[j, q * kz:(q + 1) * kz, :],
                                 preferred_element_type=jnp.float32)
            g, u = total[:, :n], total[:, n:]
            O[j, r, :] = g / (1.0 + jnp.exp(-g)) * u
            return carry

        lax.fori_loop(0, 2, tile, 0)
        out_local(j).start()
        out_sib(j, c).start()
        return carry

    def step(s, carry):
        @pl.when(s < J)
        def _():
            for k in local_copies(s):
                k.wait()
            for k in sib_copies(s, sib, 1 - c):
                k.wait_recv()
            for d in range(X - 1):
                xdirect(s, d, p).start()
            for d in range(Y - 1):
                ydirect(s, d, p).start()

        @pl.when(s + 2 < J)
        def _():
            fetch(s + 2)

        @pl.when(jnp.logical_and(s >= 1, s <= J))
        def _():
            j = s - 1
            for d in range(X - 1):
                q = chip(y, xfrom[d])
                xdirect(j, d, q).wait_recv()
                for e in range(Y - 1):
                    fwda(j, d, e, q).start()
            for e in range(Y - 1):
                q = chip(yfrom[e], x)
                ydirect(j, e, q).wait_recv()
                for d in range(X - 1):
                    fwdb(j, d, e, q).start()

        @pl.when(s == late - 1)
        def _():
            for d in range(Z - 1):
                tok_send[d].wait_recv()
                tok_fwd(d, c).start()

        @pl.when(s == late)
        def _():
            tok_local.wait()
            remote(tok, trows(z, 1 - c), tls.at[0], tlr.at[0], sib, z).wait_recv()
            for d in range(Z - 1):
                tok_fwd(d, 1 - c).wait_recv()

        lax.fori_loop(done(s - 1), done(s), compute, 0)
        return carry

    lax.fori_loop(0, J + 2, step, 0)

    tok_sib.wait_send()
    for d in range(Z - 1):
        tok_send[d].wait_send()
        tok_fwd(d, c).wait_send()

    def finish(j, carry):
        for k in sib_copies(j, row, 1 - c):
            k.wait_send()
        for d in range(X - 1):
            xdirect(j, d, p).wait_send()
            for e in range(Y - 1):
                fwda(j, d, e, chip(y, xfrom[d])).wait_send()
        for e in range(Y - 1):
            ydirect(j, e, p).wait_send()
            for d in range(X - 1):
                fwdb(j, d, e, chip(yfrom[e], x)).wait_send()
        out_local(j).wait()
        out_sib(j, c).wait_send()
        out_sib(j, 1 - c).wait_recv()
        return carry

    lax.fori_loop(0, J, finish, 0)


def grid_kernel(Y, X, Z, n, tok, gate, up, out, T, W, O, U, loc, sibs, sibr, ys, yr, xs, xr,
                tl, hs, hr, zs, zr, fs, fr, ol, osd, orv):
    rows, kz = tok.shape
    kr = gate.shape[0]
    quarter = gate.shape[1] // 4
    J = quarter // n
    kc = 2 * kr
    row, z = lax.axis_index("row"), lax.axis_index("col")
    c, p = lax.rem(row, 2), row // 2
    x, y = lax.rem(p, X), p // X
    c2, y2 = 1 - c, 1 - y

    def dev(yy, xx, cc):
        return (yy * X + xx) * 2 + cc

    def al(v, k):
        return pl.multiple_of(v, k)

    def remote(src, dst, s, r, drow, dcol):
        return pltpu.make_async_remote_copy(
            src_ref=src, dst_ref=dst, send_sem=s, recv_sem=r,
            device_id=(drow, dcol), device_id_type=MESH)

    sib, across, cross = dev(y, x, c2), dev(y2, x, c), dev(y2, x, c2)
    xpeers = [lax.rem(x + d, X) for d in range(1, X)]
    xfrom = [lax.rem(x + X - d, X) for d in range(1, X)]

    barrier = pltpu.get_barrier_semaphore()

    def greet(drow, dcol):
        pl.semaphore_signal(barrier, inc=1, device_id=(drow, dcol), device_id_type=MESH)

    for q in [sib, across, cross] + [dev(y, q, c) for q in xpeers]:
        greet(q, z)

    @pl.when(z > 0)
    def _():
        greet(row, z - 1)

    @pl.when(z < Z - 1)
    def _():
        greet(row, z + 1)

    pl.semaphore_wait(barrier, 2 + X + jnp.minimum(z, 1) + jnp.minimum(Z - 1 - z, 1))

    def cols(ref, yy, cc, j):
        return ref.at[:, pl.ds(al((yy * 2 + cc) * quarter + j * n, n), n)]

    def place(j, owner, i):
        return W.at[j, pl.ds(al(owner * kr, kr), kr), pl.ds(i * n, n)]

    def local_copies(j):
        return [pltpu.make_async_copy(cols(ref, y, c, j), place(j, row, i), loc.at[j, i])
                for i, ref in enumerate((gate, up))]

    def sib_copies(j, owner):
        return [remote(cols(ref, y, c2, j), place(j, owner, i), sibs.at[j, i], sibr.at[j, i], sib, z)
                for i, ref in enumerate((gate, up))]

    def y_copies(j, owners):
        return [remote(cols(ref, y2, cc, j), place(j, owners[k], i), ys.at[j, k, i], yr.at[j, k, i],
                       dest, z)
                for k, (cc, dest) in enumerate(((c, across), (c2, cross)))
                for i, ref in enumerate((gate, up))]

    def x_copy(j, d, k, q):
        yy = y2 if k else y
        b = W.at[j, pl.ds(al((yy * X + q) * kc, kc), kc), :]
        return remote(b, b, xs.at[j, d, k], xr.at[j, d, k], dev(y, xpeers[d], c), z)

    def fetch(j):
        for k in local_copies(j) + sib_copies(j, row):
            k.start()

    def fetch_y(j):
        for k in y_copies(j, (row, row)):
            k.start()

    def trows(q, t, core):
        return T.at[q, pl.ds(al(((y if t else y2) * 2 + core) * rows, rows), rows), :]

    tok_local = pltpu.make_async_copy(tok, trows(z, 1, c), tl.at[0])
    tok_y = remote(tok, trows(z, 1, c), hs.at[0], hr.at[0], across, z)
    tok_y_in = remote(tok, trows(z, 0, c), hs.at[0], hr.at[0], across, z)
    tok_sib = remote(tok, trows(z, 1, c), hs.at[1], hr.at[1], sib, z)
    tok_sib_in = remote(tok, trows(z, 1, c2), hs.at[1], hr.at[1], sib, z)

    def pair_sib(core):
        return remote(trows(z, 0, core), trows(z, 0, core), hs.at[2], hr.at[2], sib, z)

    def hop(t, h, up_way, q):
        w = 0 if up_way else 1
        dst = z + 1 if up_way else z - 1
        src = tok if (t == 1 and h == 1) else trows(q, t, c)
        return remote(src, trows(q, t, c), zs.at[t, h - 1, w], zr.at[t, h - 1, w], row, dst)

    def has_send(h, up_way):
        return (jnp.logical_and(z >= h - 1, z < Z - 1) if up_way
                else jnp.logical_and(z <= Z - h, z > 0))

    def has_recv(h, up_way):
        return z >= h if up_way else z < Z - h

    def hop_send(t, h, wait=False):
        for up_way in (True, False):
            @pl.when(has_send(h, up_way))
            def _():
                q = z - (h - 1) if up_way else z + (h - 1)
                k = hop(t, h, up_way, q)
                if wait:
                    k.wait_send()
                else:
                    k.start()

    def to_sib(t, h, up_way, core):
        q = z - h if up_way else z + h
        w = 0 if up_way else 1
        return remote(trows(q, t, core), trows(q, t, core), fs.at[t, h - 1, w], fr.at[t, h - 1, w], sib, z)

    def hop_recv(t, h):
        for up_way in (True, False):
            @pl.when(has_recv(h, up_way))
            def _():
                q = z - h if up_way else z + h
                hop(t, h, up_way, q).wait_recv()
                to_sib(t, h, up_way, c).start()

            if h < Z - 1:
                @pl.when(has_send(h + 1, up_way))
                def _():
                    hop(t, h + 1, up_way, z - h if up_way else z + h).start()

    def sib_wait(t, send, first, last):
        for h in range(first, last + 1):
            for up_way in (True, False):
                @pl.when(has_recv(h, up_way))
                def _():
                    if send:
                        to_sib(t, h, up_way, c).wait_send()
                    else:
                        to_sib(t, h, up_way, c2).wait_recv()

    def orows(j, yy, cc):
        return O.at[j, pl.ds(al((yy * 2 + cc) * rows, rows), rows), :]

    def out_local(j):
        return pltpu.make_async_copy(orows(j, y, c), cols(out, y, c, j), ol.at[j])

    def out_copy(j, k, incoming=False):
        yy, cc, dest = ((y, c2, sib), (y2, c, across), (y2, c2, cross))[k]
        fy, fc = (yy, cc) if incoming else (y, c)
        return remote(orows(j, yy, cc), cols(out, fy, fc, j), osd.at[j, k], orv.at[j, k], dest, z)

    def tiles(j, yy):
        def tile(m, carry):
            r = pl.ds(al((yy * 2 + m) * rows, rows), rows)
            total = jnp.zeros((rows, 2 * n), jnp.float32)
            for q in range(Z):
                total += jnp.dot(T[q, r, :], W[j, q * kz:(q + 1) * kz, :],
                                 preferred_element_type=jnp.float32)
            g, u = total[:, :n], total[:, n:]
            O[j, r, :] = g / (1.0 + jnp.exp(-g)) * u
            return carry

        lax.fori_loop(0, 2, tile, 0)

    far_z = jnp.where(z < Z // 2, Z - 1, 0)
    near_first = jnp.where(z < Z // 2, 0, 1)

    def slab(j, r, q):
        return jnp.dot(T[q, r, :], W[j, pl.ds(al(q * kz, kz), kz), :],
                       preferred_element_type=jnp.float32)

    def own_near(j, carry):
        def tile(m, carry):
            r = pl.ds(al((y * 2 + m) * rows, rows), rows)
            total = slab(j, r, near_first)
            for i in range(1, Z - 1):
                total += slab(j, r, near_first + i)
            O[j, r, :] = total[:, :n]
            U[j, pl.ds(al(m * rows, rows), rows), :] = total[:, n:]
            return carry

        lax.fori_loop(0, 2, tile, 0)
        return carry

    def own_far(j, carry):
        def tile(m, carry):
            r = pl.ds(al((y * 2 + m) * rows, rows), rows)
            total = slab(j, r, far_z)
            g = O[j, r, :] + total[:, :n]
            u = U[j, pl.ds(al(m * rows, rows), rows), :] + total[:, n:]
            O[j, r, :] = g / (1.0 + jnp.exp(-g)) * u
            return carry

        lax.fori_loop(0, 2, tile, 0)
        out_local(j).start()
        out_copy(j, 0).start()
        return carry

    def compute_pair(j, carry):
        tiles(j, y2)
        out_copy(j, 1).start()
        out_copy(j, 2).start()
        return carry

    lead = min(3, J)
    tok_y.start()
    hop_send(1, 1)
    fetch(0)
    fetch_y(0)
    tok_local.start()
    tok_sib.start()
    for j in range(1, lead):
        fetch(j)

    def done(s):
        return jnp.where(s < Z - 1, 0, s)

    def send_own(j, carry):
        for k in local_copies(j):
            k.wait()
        for k in sib_copies(j, sib):
            k.wait_recv()
        for d in range(X - 1):
            x_copy(j, d, 0, x).start()
        return carry

    def step(s, carry):
        lax.fori_loop(jnp.where(s == 0, 0, s + lead - 1), jnp.minimum(s + lead, J), send_own, 0)

        @pl.when(s + lead < J)
        def _():
            fetch(s + lead)

        @pl.when(s == 0)
        def _():
            tok_y_in.wait_recv()
            hop_send(0, 1)
            pair_sib(c).start()
            fetch_y(1)

        @pl.when(s + 2 < J)
        def _():
            fetch_y(s + 2)

        @pl.when(s < J)
        def _():
            for k in y_copies(s, (across, cross)):
                k.wait_recv()
            for d in range(X - 1):
                x_copy(s, d, 1, x).start()

        for h in range(1, Z):
            @pl.when(s == h)
            def _():
                hop_recv(0, h)

        for h in range(1, Z - 1):
            @pl.when(s == Z - 2 + h)
            def _():
                hop_recv(1, h)

        @pl.when(s == Z - 1)
        def _():
            pair_sib(c2).wait_recv()
            sib_wait(0, False, 1, Z - 1)

        lax.fori_loop(jnp.where(s == J, J - 2, 0), jnp.where(s == J, J - 1, 0), own_near, 0)

        @pl.when(s >= 1)
        def _():
            for d in range(X - 1):
                for k in range(2):
                    x_copy(s - 1, d, k, xfrom[d]).wait_recv()

        lax.fori_loop(done(s - 1), done(s), compute_pair, 0)

        @pl.when(s == J - 1)
        def _():
            tok_local.wait()
            tok_sib_in.wait_recv()
            sib_wait(1, False, 1, Z - 2)

        @pl.when(s == J)
        def _():
            hop_recv(1, Z - 1)

        lax.fori_loop(jnp.where(s == J, J - 1, 0), jnp.where(s == J, J, jnp.where(s == J - 1, J - 2, 0)),
                      own_near, 0)
        return carry

    lax.fori_loop(0, J + 1, step, 0)
    sib_wait(1, False, Z - 1, Z - 1)
    lax.fori_loop(0, J, own_far, 0)

    tok_y.wait_send()
    tok_sib.wait_send()
    pair_sib(c).wait_send()
    for t in range(2):
        sib_wait(t, True, 1, Z - 1)
        for h in range(1, Z):
            hop_send(t, h, wait=True)

    def finish(j, carry):
        for k in sib_copies(j, row) + y_copies(j, (row, row)):
            k.wait_send()
        for d in range(X - 1):
            for k in range(2):
                x_copy(j, d, k, x).wait_send()
        out_local(j).wait()
        for k in range(3):
            out_copy(j, k).wait_send()
            out_copy(j, k, True).wait_recv()
        return carry

    lax.fori_loop(0, J, finish, 0)


def solution(mesh):
    R, Z = mesh.shape["row"], mesh.shape["col"]
    chips = R // 2
    Y = 2 if chips % 2 == 0 else 1
    X = chips // Y

    def per_device(tokens, gate_weight, up_weight):
        rows, kz = tokens.shape
        kr, cols = gate_weight.shape
        n = 128
        half = cols // 2
        J = half // n
        dma = pltpu.SemaphoreType.DMA
        ux, uy, uz = max(X - 1, 1), max(Y - 1, 1), max(Z - 1, 1)
        quarter = cols // 4
        grid = Y == 2 and Z > 2 and quarter % n == 0 and quarter // n >= 2 * Z - 2
        scratch = [
            pltpu.VMEM((Z, 2 * rows, kz), jnp.bfloat16),
            pltpu.VMEM((J, R * kr, 2 * n), jnp.bfloat16),
            pltpu.VMEM((J, 2 * rows, n), jnp.float32),
            dma((J, 2)), dma((J, 2)), dma((J, 2)),
            dma((1,)), dma((1,)), dma((uz,)), dma((uz,)), dma((uz,)), dma((uz,)),
            dma((J, ux)), dma((J, ux)), dma((J, uy)), dma((J, uy)),
            dma((J, ux, uy)), dma((J, ux, uy)), dma((J, ux, uy)), dma((J, ux, uy)),
            dma((J,)), dma((J,)), dma((J,)), dma((1,)),
        ]
        if grid:
            J = quarter // n
            scratch = [
                pltpu.VMEM((Z, 4 * rows, kz), jnp.bfloat16),
                pltpu.VMEM((J, R * kr, 2 * n), jnp.bfloat16),
                pltpu.VMEM((J, 4 * rows, n), jnp.float32),
                pltpu.VMEM((J, 2 * rows, n), jnp.float32),
                dma((J, 2)), dma((J, 2)), dma((J, 2)), dma((J, 2, 2)), dma((J, 2, 2)),
                dma((J, ux, 2)), dma((J, ux, 2)), dma((1,)), dma((3,)), dma((3,)),
                dma((2, uz, 2)), dma((2, uz, 2)), dma((2, uz, 2)), dma((2, uz, 2)),
                dma((J,)), dma((J, 3)), dma((J, 3)),
            ]
        return pl.pallas_call(
            functools.partial(grid_kernel if grid else kernel, Y, X, Z, n),
            out_shape=jax.ShapeDtypeStruct((rows, cols), jnp.float32),
            in_specs=[pl.BlockSpec(memory_space=pl.ANY)] * 3,
            out_specs=pl.BlockSpec(memory_space=pl.ANY),
            scratch_shapes=scratch,
            compiler_params=pltpu.CompilerParams(
                collective_id=0, has_side_effects=True, vmem_limit_bytes=62 * 2**20),
            cost_estimate=pl.CostEstimate(
                flops=4 * rows * R * kr * cols, bytes_accessed=4 * rows * cols,
                transcendentals=rows * cols),
        )(tokens, gate_weight, up_weight)

    return jax.shard_map(
        per_device, mesh=mesh, in_specs=(P("row", "col"),) * 3,
        out_specs=P("row", "col"), check_vma=False)
```

```python
import functools

import jax
import jax.numpy as jnp
from jax import lax
from jax.experimental import pallas as pl
from jax.experimental.pallas import tpu as pltpu
from jax.sharding import PartitionSpec as P

MESH = pl.DeviceIdType.MESH


def kernel(Y, X, Z, n, tok, gate, up, out, T, W, O, loc, sibs, sibr, tls, tlr, ts, tr, tfs, tfr,
           xs, xr, ys, yr, fas, far, fbs, fbr, ol, osd, orv, tl):
    rows, kz = tok.shape
    kr = gate.shape[0]
    half = gate.shape[1] // 2
    J = half // n
    row, z = lax.axis_index("row"), lax.axis_index("col")
    c, p = lax.rem(row, 2), row // 2
    x, y = lax.rem(p, X), p // X
    sib = row + 1 - 2 * c
    kc = 2 * kr

    def chip(yy, xx):
        return yy * X + xx

    def al(v, k):
        return pl.multiple_of(v, k)

    def remote(src, dst, s, r, drow, dcol):
        return pltpu.make_async_remote_copy(
            src_ref=src, dst_ref=dst, send_sem=s, recv_sem=r,
            device_id=(drow, dcol), device_id_type=MESH)

    def block(j, q):
        return W.at[j, pl.ds(al(q * kc, kc), kc), :]

    def part(j, q, h):
        return W.at[j, pl.ds(al(q * kc + h * kr, kr), kr), :]

    xpeers = [lax.rem(x + d, X) for d in range(1, X)]
    xfrom = [lax.rem(x + X - d, X) for d in range(1, X)]
    ypeers = [lax.rem(y + d, Y) for d in range(1, Y)]
    yfrom = [lax.rem(y + Y - d, Y) for d in range(1, Y)]
    zpeers = [lax.rem(z + d, Z) for d in range(1, Z)]
    zfrom = [lax.rem(z + Z - d, Z) for d in range(1, Z)]

    barrier = pltpu.get_barrier_semaphore()
    peers = [(sib, z)] + [(row, q) for q in zpeers]
    peers += [(chip(y, q) * 2 + c, z) for q in xpeers]
    peers += [(chip(q, x) * 2 + c, z) for q in ypeers]
    for q in peers:
        pl.semaphore_signal(barrier, inc=1, device_id=q, device_id_type=MESH)
    pl.semaphore_wait(barrier, len(peers))

    def local_copies(j):
        return [
            pltpu.make_async_copy(
                ref.at[:, pl.ds(al(c * half + j * n, n), n)],
                W.at[j, pl.ds(al(row * kr, kr), kr), pl.ds(i * n, n)],
                loc.at[j, i])
            for i, ref in enumerate((gate, up))]

    def sib_copies(j, owner, other):
        return [
            remote(
                ref.at[:, pl.ds(al(other * half + j * n, n), n)],
                W.at[j, pl.ds(al(owner * kr, kr), kr), pl.ds(i * n, n)],
                sibs.at[j, i], sibr.at[j, i], sib, z)
            for i, ref in enumerate((gate, up))]

    def fetch(j):
        for k in local_copies(j) + sib_copies(j, row, 1 - c):
            k.start()

    def xdirect(j, d, q):
        return remote(block(j, q), block(j, q), xs.at[j, d], xr.at[j, d],
                      chip(y, xpeers[d]) * 2 + c, z)

    def ydirect(j, d, q):
        return remote(block(j, q), block(j, q), ys.at[j, d], yr.at[j, d],
                      chip(ypeers[d], x) * 2 + c, z)

    def fwda(j, dx, dy, q):
        return remote(part(j, q, 0), part(j, q, 0), fas.at[j, dx, dy], far.at[j, dx, dy],
                      chip(ypeers[dy], x) * 2 + c, z)

    def fwdb(j, dx, dy, q):
        return remote(part(j, q, 1), part(j, q, 1), fbs.at[j, dx, dy], fbr.at[j, dx, dy],
                      chip(y, xpeers[dx]) * 2 + c, z)

    def trows(q, core):
        return T.at[q, pl.ds(al(core * rows, rows), rows), :]

    tok_local = pltpu.make_async_copy(tok, trows(z, c), tl.at[0])
    tok_sib = remote(tok, trows(z, c), tls.at[0], tlr.at[0], sib, z)
    tok_send = [remote(tok, trows(z, c), ts.at[d], tr.at[d], row, zpeers[d]) for d in range(Z - 1)]

    def tok_fwd(d, core):
        return remote(trows(zfrom[d], core), trows(zfrom[d], core), tfs.at[d], tfr.at[d], sib, z)

    def out_local(j):
        return pltpu.make_async_copy(
            O.at[j, pl.ds(al(c * rows, rows), rows), :],
            out.at[:, pl.ds(al(c * half + j * n, n), n)], ol.at[j])

    def out_sib(j, core):
        return remote(
            O.at[j, pl.ds(al((1 - c) * rows, rows), rows), :],
            out.at[:, pl.ds(al(core * half + j * n, n), n)], osd.at[j], orv.at[j], sib, z)

    fetch(0)
    for k in tok_send:
        k.start()
    if J > 1:
        fetch(1)
    tok_local.start()
    tok_sib.start()

    late = (J + 1) // 2

    def done(s):
        return jnp.maximum(jnp.minimum(s - 1, 2 * (s - late + 1)), 0)

    def compute(j, carry):
        for d in range(X - 1):
            for e in range(Y - 1):
                q = chip(yfrom[e], xfrom[d])
                fwda(j, d, e, q).wait_recv()
                fwdb(j, d, e, q).wait_recv()

        def tile(m, carry):
            r = pl.ds(al(m * rows, rows), rows)
            total = jnp.zeros((rows, 2 * n), jnp.float32)
            for q in range(Z):
                total += jnp.dot(T[q, r, :], W[j, q * kz:(q + 1) * kz, :],
                                 preferred_element_type=jnp.float32)
            g, u = total[:, :n], total[:, n:]
            O[j, r, :] = g / (1.0 + jnp.exp(-g)) * u
            return carry

        lax.fori_loop(0, 2, tile, 0)
        out_local(j).start()
        out_sib(j, c).start()
        return carry

    def step(s, carry):
        @pl.when(s < J)
        def _():
            for k in local_copies(s):
                k.wait()
            for k in sib_copies(s, sib, 1 - c):
                k.wait_recv()
            for d in range(X - 1):
                xdirect(s, d, p).start()
            for d in range(Y - 1):
                ydirect(s, d, p).start()

        @pl.when(s + 2 < J)
        def _():
            fetch(s + 2)

        @pl.when(jnp.logical_and(s >= 1, s <= J))
        def _():
            j = s - 1
            for d in range(X - 1):
                q = chip(y, xfrom[d])
                xdirect(j, d, q).wait_recv()
                for e in range(Y - 1):
                    fwda(j, d, e, q).start()
            for e in range(Y - 1):
                q = chip(yfrom[e], x)
                ydirect(j, e, q).wait_recv()
                for d in range(X - 1):
                    fwdb(j, d, e, q).start()

        @pl.when(s == late - 1)
        def _():
            for d in range(Z - 1):
                tok_send[d].wait_recv()
                tok_fwd(d, c).start()

        @pl.when(s == late)
        def _():
            tok_local.wait()
            remote(tok, trows(z, 1 - c), tls.at[0], tlr.at[0], sib, z).wait_recv()
            for d in range(Z - 1):
                tok_fwd(d, 1 - c).wait_recv()

        lax.fori_loop(done(s - 1), done(s), compute, 0)
        return carry

    lax.fori_loop(0, J + 2, step, 0)

    tok_sib.wait_send()
    for d in range(Z - 1):
        tok_send[d].wait_send()
        tok_fwd(d, c).wait_send()

    def finish(j, carry):
        for k in sib_copies(j, row, 1 - c):
            k.wait_send()
        for d in range(X - 1):
            xdirect(j, d, p).wait_send()
            for e in range(Y - 1):
                fwda(j, d, e, chip(y, xfrom[d])).wait_send()
        for e in range(Y - 1):
            ydirect(j, e, p).wait_send()
            for d in range(X - 1):
                fwdb(j, d, e, chip(yfrom[e], x)).wait_send()
        out_local(j).wait()
        out_sib(j, c).wait_send()
        out_sib(j, 1 - c).wait_recv()
        return carry

    lax.fori_loop(0, J, finish, 0)


def grid_kernel(Y, X, Z, n, tok, gate, up, out, T, W, O, U, loc, sibs, sibr, ys, yr, xs, xr,
                tl, hs, hr, zs, zr, fs, fr, ol, osd, orv):
    rows, kz = tok.shape
    kr = gate.shape[0]
    quarter = gate.shape[1] // 4
    J = quarter // n
    kc = 2 * kr
    row, z = lax.axis_index("row"), lax.axis_index("col")
    c, p = lax.rem(row, 2), row // 2
    x, y = lax.rem(p, X), p // X
    c2, y2 = 1 - c, 1 - y

    def dev(yy, xx, cc):
        return (yy * X + xx) * 2 + cc

    def al(v, k):
        return pl.multiple_of(v, k)

    def remote(src, dst, s, r, drow, dcol):
        return pltpu.make_async_remote_copy(
            src_ref=src, dst_ref=dst, send_sem=s, recv_sem=r,
            device_id=(drow, dcol), device_id_type=MESH)

    sib, across, cross = dev(y, x, c2), dev(y2, x, c), dev(y2, x, c2)
    xpeers = [lax.rem(x + d, X) for d in range(1, X)]
    xfrom = [lax.rem(x + X - d, X) for d in range(1, X)]

    barrier = pltpu.get_barrier_semaphore()

    def greet(drow, dcol):
        pl.semaphore_signal(barrier, inc=1, device_id=(drow, dcol), device_id_type=MESH)

    for q in [sib, across, cross] + [dev(y, q, c) for q in xpeers]:
        greet(q, z)

    @pl.when(z > 0)
    def _():
        greet(row, z - 1)

    @pl.when(z < Z - 1)
    def _():
        greet(row, z + 1)

    pl.semaphore_wait(barrier, 2 + X + jnp.minimum(z, 1) + jnp.minimum(Z - 1 - z, 1))

    def cols(ref, yy, cc, j):
        return ref.at[:, pl.ds(al((yy * 2 + cc) * quarter + j * n, n), n)]

    def place(j, owner, i):
        return W.at[j, pl.ds(al(owner * kr, kr), kr), pl.ds(i * n, n)]

    def local_copies(j):
        return [pltpu.make_async_copy(cols(ref, y, c, j), place(j, row, i), loc.at[j, i])
                for i, ref in enumerate((gate, up))]

    def sib_copies(j, owner):
        return [remote(cols(ref, y, c2, j), place(j, owner, i), sibs.at[j, i], sibr.at[j, i], sib, z)
                for i, ref in enumerate((gate, up))]

    def y_copies(j, owners):
        return [remote(cols(ref, y2, cc, j), place(j, owners[k], i), ys.at[j, k, i], yr.at[j, k, i],
                       dest, z)
                for k, (cc, dest) in enumerate(((c, across), (c2, cross)))
                for i, ref in enumerate((gate, up))]

    def x_copy(j, d, k, q):
        yy = y2 if k else y
        b = W.at[j, pl.ds(al((yy * X + q) * kc, kc), kc), :]
        return remote(b, b, xs.at[j, d, k], xr.at[j, d, k], dev(y, xpeers[d], c), z)

    def fetch(j):
        for k in local_copies(j) + sib_copies(j, row):
            k.start()

    def fetch_y(j):
        for k in y_copies(j, (row, row)):
            k.start()

    def trows(q, t, core):
        return T.at[q, pl.ds(al(((y if t else y2) * 2 + core) * rows, rows), rows), :]

    tok_local = pltpu.make_async_copy(tok, trows(z, 1, c), tl.at[0])
    tok_y = remote(tok, trows(z, 1, c), hs.at[0], hr.at[0], across, z)
    tok_y_in = remote(tok, trows(z, 0, c), hs.at[0], hr.at[0], across, z)
    tok_sib = remote(tok, trows(z, 1, c), hs.at[1], hr.at[1], sib, z)
    tok_sib_in = remote(tok, trows(z, 1, c2), hs.at[1], hr.at[1], sib, z)

    def pair_sib(core):
        return remote(trows(z, 0, core), trows(z, 0, core), hs.at[2], hr.at[2], sib, z)

    def hop(t, h, up_way, q):
        w = 0 if up_way else 1
        dst = z + 1 if up_way else z - 1
        src = tok if (t == 1 and h == 1) else trows(q, t, c)
        return remote(src, trows(q, t, c), zs.at[t, h - 1, w], zr.at[t, h - 1, w], row, dst)

    def has_send(h, up_way):
        return (jnp.logical_and(z >= h - 1, z < Z - 1) if up_way
                else jnp.logical_and(z <= Z - h, z > 0))

    def has_recv(h, up_way):
        return z >= h if up_way else z < Z - h

    def hop_send(t, h, wait=False):
        for up_way in (True, False):
            @pl.when(has_send(h, up_way))
            def _():
                q = z - (h - 1) if up_way else z + (h - 1)
                k = hop(t, h, up_way, q)
                if wait:
                    k.wait_send()
                else:
                    k.start()

    def to_sib(t, h, up_way, core):
        q = z - h if up_way else z + h
        w = 0 if up_way else 1
        return remote(trows(q, t, core), trows(q, t, core), fs.at[t, h - 1, w], fr.at[t, h - 1, w], sib, z)

    def hop_recv(t, h):
        for up_way in (True, False):
            @pl.when(has_recv(h, up_way))
            def _():
                q = z - h if up_way else z + h
                hop(t, h, up_way, q).wait_recv()
                to_sib(t, h, up_way, c).start()

            if h < Z - 1:
                @pl.when(has_send(h + 1, up_way))
                def _():
                    hop(t, h + 1, up_way, z - h if up_way else z + h).start()

    def sib_wait(t, send, first, last):
        for h in range(first, last + 1):
            for up_way in (True, False):
                @pl.when(has_recv(h, up_way))
                def _():
                    if send:
                        to_sib(t, h, up_way, c).wait_send()
                    else:
                        to_sib(t, h, up_way, c2).wait_recv()

    def orows(j, yy, cc):
        return O.at[j, pl.ds(al((yy * 2 + cc) * rows, rows), rows), :]

    def out_local(j):
        return pltpu.make_async_copy(orows(j, y, c), cols(out, y, c, j), ol.at[j])

    def out_copy(j, k, incoming=False):
        yy, cc, dest = ((y, c2, sib), (y2, c, across), (y2, c2, cross))[k]
        fy, fc = (yy, cc) if incoming else (y, c)
        return remote(orows(j, yy, cc), cols(out, fy, fc, j), osd.at[j, k], orv.at[j, k], dest, z)

    def tiles(j, yy):
        def tile(m, carry):
            r = pl.ds(al((yy * 2 + m) * rows, rows), rows)
            total = jnp.zeros((rows, 2 * n), jnp.float32)
            for q in range(Z):
                total += jnp.dot(T[q, r, :], W[j, q * kz:(q + 1) * kz, :],
                                 preferred_element_type=jnp.float32)
            g, u = total[:, :n], total[:, n:]
            O[j, r, :] = g / (1.0 + jnp.exp(-g)) * u
            return carry

        lax.fori_loop(0, 2, tile, 0)

    far_z = jnp.where(z < Z // 2, Z - 1, 0)
    near_first = jnp.where(z < Z // 2, 0, 1)

    def slab(j, r, q):
        return jnp.dot(T[q, r, :], W[j, pl.ds(al(q * kz, kz), kz), :],
                       preferred_element_type=jnp.float32)

    def own_near(j, carry):
        def tile(m, carry):
            r = pl.ds(al((y * 2 + m) * rows, rows), rows)
            total = slab(j, r, near_first)
            for i in range(1, Z - 1):
                total += slab(j, r, near_first + i)
            O[j, r, :] = total[:, :n]
            U[j, pl.ds(al(m * rows, rows), rows), :] = total[:, n:]
            return carry

        lax.fori_loop(0, 2, tile, 0)
        return carry

    def own_far(j, carry):
        def tile(m, carry):
            r = pl.ds(al((y * 2 + m) * rows, rows), rows)
            total = slab(j, r, far_z)
            g = O[j, r, :] + total[:, :n]
            u = U[j, pl.ds(al(m * rows, rows), rows), :] + total[:, n:]
            O[j, r, :] = g / (1.0 + jnp.exp(-g)) * u
            return carry

        lax.fori_loop(0, 2, tile, 0)
        out_local(j).start()
        out_copy(j, 0).start()
        return carry

    def compute_pair(j, carry):
        tiles(j, y2)
        out_copy(j, 1).start()
        out_copy(j, 2).start()
        return carry

    split = X == 2 and Z == X * Y
    early = [y * X + x, y2 * X + x, y * X + xfrom[0]]

    def last_near(m, carry):
        r = pl.ds(al((y2 * 2 + m) * rows, rows), rows)
        total = slab(J - 1, r, early[0])
        for q in early[1:]:
            total += slab(J - 1, r, q)
        O[J - 1, r, :] = total[:, :n]
        U[J, pl.ds(al(m * rows, rows), rows), :] = total[:, n:]
        return carry

    def last_far(m):
        r = pl.ds(al((y2 * 2 + m) * rows, rows), rows)
        total = slab(J - 1, r, y2 * X + xfrom[0])
        g = O[J - 1, r, :] + total[:, :n]
        u = U[J, pl.ds(al(m * rows, rows), rows), :] + total[:, n:]
        O[J - 1, r, :] = g / (1.0 + jnp.exp(-g)) * u

    lead = min(3, J)
    tok_y.start()
    hop_send(1, 1)
    fetch(0)
    fetch_y(0)
    tok_local.start()
    tok_sib.start()
    for j in range(1, lead):
        fetch(j)

    def done(s):
        return jnp.where(s < Z - 1, 0, s)

    def send_own(j, carry):
        for k in local_copies(j):
            k.wait()
        for k in sib_copies(j, sib):
            k.wait_recv()
        for d in range(X - 1):
            x_copy(j, d, 0, x).start()
        return carry

    def step(s, carry):
        lax.fori_loop(jnp.where(s == 0, 0, s + lead - 1), jnp.minimum(s + lead, J), send_own, 0)

        @pl.when(s + lead < J)
        def _():
            fetch(s + lead)

        @pl.when(s == 0)
        def _():
            tok_y_in.wait_recv()
            hop_send(0, 1)
            pair_sib(c).start()
            fetch_y(1)

        @pl.when(s + 2 < J)
        def _():
            fetch_y(s + 2)

        @pl.when(s < J)
        def _():
            for k in y_copies(s, (across, cross)):
                k.wait_recv()
            for d in range(X - 1):
                x_copy(s, d, 1, x).start()

        for h in range(1, Z):
            @pl.when(s == h)
            def _():
                hop_recv(0, h)

        for h in range(1, Z - 1):
            @pl.when(s == Z - 2 + h)
            def _():
                hop_recv(1, h)

        @pl.when(s == Z - 1)
        def _():
            pair_sib(c2).wait_recv()
            sib_wait(0, False, 1, Z - 1)

        lax.fori_loop(jnp.where(s == J, J - 2, 0), jnp.where(s == J, J - 1, 0), own_near, 0)

        @pl.when(s >= 1)
        def _():
            for d in range(X - 1):
                x_copy(s - 1, d, 0, xfrom[d]).wait_recv()

        if split:
            lax.fori_loop(0, jnp.where(s == J, 2, 0), last_near, 0)

        @pl.when(s >= 1)
        def _():
            for d in range(X - 1):
                x_copy(s - 1, d, 1, xfrom[d]).wait_recv()

        if split:
            @pl.when(s == J)
            def _():
                last_far(c)
                out_copy(J - 1, 1).start()
                last_far(c2)
                out_copy(J - 1, 2).start()

        lax.fori_loop(done(s - 1), jnp.minimum(done(s), J - 1 if split else J), compute_pair, 0)

        @pl.when(s == J - 1)
        def _():
            tok_local.wait()
            tok_sib_in.wait_recv()
            sib_wait(1, False, 1, Z - 2)

        @pl.when(s == J)
        def _():
            hop_recv(1, Z - 1)

        lax.fori_loop(jnp.where(s == J, J - 1, 0), jnp.where(s == J, J, jnp.where(s == J - 1, J - 2, 0)),
                      own_near, 0)
        return carry

    lax.fori_loop(0, J + 1, step, 0)
    sib_wait(1, False, Z - 1, Z - 1)
    lax.fori_loop(0, J, own_far, 0)

    tok_y.wait_send()
    tok_sib.wait_send()
    pair_sib(c).wait_send()
    for t in range(2):
        sib_wait(t, True, 1, Z - 1)
        for h in range(1, Z):
            hop_send(t, h, wait=True)

    def finish(j, carry):
        for k in sib_copies(j, row) + y_copies(j, (row, row)):
            k.wait_send()
        for d in range(X - 1):
            for k in range(2):
                x_copy(j, d, k, x).wait_send()
        out_local(j).wait()
        for k in range(3):
            out_copy(j, k).wait_send()
            out_copy(j, k, True).wait_recv()
        return carry

    lax.fori_loop(0, J, finish, 0)


def solution(mesh):
    R, Z = mesh.shape["row"], mesh.shape["col"]
    chips = R // 2
    Y = 2 if chips % 2 == 0 else 1
    X = chips // Y

    def per_device(tokens, gate_weight, up_weight):
        rows, kz = tokens.shape
        kr, cols = gate_weight.shape
        n = 128
        half = cols // 2
        J = half // n
        dma = pltpu.SemaphoreType.DMA
        ux, uy, uz = max(X - 1, 1), max(Y - 1, 1), max(Z - 1, 1)
        quarter = cols // 4
        grid = Y == 2 and Z > 2 and quarter % n == 0 and quarter // n >= 2 * Z - 2
        scratch = [
            pltpu.VMEM((Z, 2 * rows, kz), jnp.bfloat16),
            pltpu.VMEM((J, R * kr, 2 * n), jnp.bfloat16),
            pltpu.VMEM((J, 2 * rows, n), jnp.float32),
            dma((J, 2)), dma((J, 2)), dma((J, 2)),
            dma((1,)), dma((1,)), dma((uz,)), dma((uz,)), dma((uz,)), dma((uz,)),
            dma((J, ux)), dma((J, ux)), dma((J, uy)), dma((J, uy)),
            dma((J, ux, uy)), dma((J, ux, uy)), dma((J, ux, uy)), dma((J, ux, uy)),
            dma((J,)), dma((J,)), dma((J,)), dma((1,)),
        ]
        if grid:
            J = quarter // n
            scratch = [
                pltpu.VMEM((Z, 4 * rows, kz), jnp.bfloat16),
                pltpu.VMEM((J, R * kr, 2 * n), jnp.bfloat16),
                pltpu.VMEM((J, 4 * rows, n), jnp.float32),
                pltpu.VMEM((J + 1, 2 * rows, n), jnp.float32),
                dma((J, 2)), dma((J, 2)), dma((J, 2)), dma((J, 2, 2)), dma((J, 2, 2)),
                dma((J, ux, 2)), dma((J, ux, 2)), dma((1,)), dma((3,)), dma((3,)),
                dma((2, uz, 2)), dma((2, uz, 2)), dma((2, uz, 2)), dma((2, uz, 2)),
                dma((J,)), dma((J, 3)), dma((J, 3)),
            ]
        return pl.pallas_call(
            functools.partial(grid_kernel if grid else kernel, Y, X, Z, n),
            out_shape=jax.ShapeDtypeStruct((rows, cols), jnp.float32),
            in_specs=[pl.BlockSpec(memory_space=pl.ANY)] * 3,
            out_specs=pl.BlockSpec(memory_space=pl.ANY),
            scratch_shapes=scratch,
            compiler_params=pltpu.CompilerParams(
                collective_id=0, has_side_effects=True, vmem_limit_bytes=62 * 2**20),
            cost_estimate=pl.CostEstimate(
                flops=4 * rows * R * kr * cols, bytes_accessed=4 * rows * cols,
                transcendentals=rows * cols),
        )(tokens, gate_weight, up_weight)

    return jax.shard_map(
        per_device, mesh=mesh, in_specs=(P("row", "col"),) * 3,
        out_specs=P("row", "col"), check_vma=False)
```
